256 devices in a mesh: row: 32 (over z_hi, y, core), col: 8 (over z_lo, x).
Axes of the slice: x: 4, y: 4, z: 8 (z_hi: 4, z_lo: 2; z = z_hi * 2 + z_lo), core: 2. Of those that a mesh axis runs over, the one named last changes fastest.
Arguments:
- window: float32 [16384, 8192], P('row', 'col'), may hold values from -6 to 6
- left_slots: float32 [32, 8, 2, 1, 512, 512], P('row', 'col'), may hold values from -0.25 to 0.25
- right_slots: float32 [32, 8, 2, 2, 512, 512], P('row', 'col'), may hold values from -0.25 to 0.25
- left_owner: int32 [32, 2], P('row'), may hold values from 0 to 7
- right_owner: int32 [8, 2], P('col'), may hold values from 0 to 31
Outputs:
- updated: float32 [16384, 8192], P('row', 'col')
The draws below stay inside these ranges and needn't reach their ends.
Inputs may be any that keep to these rules, and one draw needn't show every extreme that they name: Only the slot of the device at tile row i and tile column left_owner[i, s] is read for section s of tile row i. Only the slot of the device at tile row right_owner[j, s] and tile column j is read for section s of tile column j.
All inputs are finite; a program needn't handle non-finite values.
Results may differ from the reference program's by a relative error of at most 0.000071.
Values sent between devices are 32-bit elements; how exact they have to be, the bound alone decides.
A program may use at most 64 MiB of HBM per device.

```python
import jax
import jax.numpy as jnp
from jax import lax

B = 512
TR = 512
TC = 1024
NR = 16384
NC = 8192
N_ROW = 32
N_COL = 8


def with_ends(entries, stream_key, least, largest):
    longest = entries.shape.index(max(entries.shape))
    spots = []
    for shift in (0, 1):
        where = [jax.random.randint(jax.random.fold_in(stream_key, axis), (), 0, length) for axis, length in enumerate(entries.shape)]
        where[longest] = (where[longest] + shift) % entries.shape[longest]
        spots.append(tuple(where))
    return entries.at[spots[0]].set(least).at[spots[1]].set(largest)


def level_of(rng, extent, cuts, least, top_value):
    def one(position, blocks):
        heights = jax.random.uniform(jax.random.fold_in(jax.random.fold_in(rng, 6), position), (blocks,), jnp.float32, least / len(cuts), top_value / len(cuts))
        return jnp.repeat(jnp.exp(heights), extent[position] // blocks).reshape((-1,) + (1,) * (len(extent) - position - 1))

    gain = one(*cuts[0])
    for cut in cuts[1:]:
        gain = gain * one(*cut)
    return gain


def normal_values(own_key, dims, spread, reach, split=(), kind=jnp.bfloat16):
    values = spread * jax.random.normal(own_key, dims, jnp.float32)
    if split:
        values = values * level_of(own_key, dims, split, -0.22, 0.18)
    return jnp.clip(values, -reach, reach).astype(kind)


def setup_inputs(seed: int = 0) -> dict:
    splits = jax.random.split(jax.random.key(seed), 6)
    window = normal_values(splits[0], (NR, NC), 1.0, 6.0, ((0, 32), (1, 8)), jnp.float32)
    left_slots = normal_values(splits[1], (N_ROW, N_COL, 2, TR // B, B, B), B ** -0.5, 0.25, ((0, 32), (1, 8)), jnp.float32)
    right_slots = normal_values(splits[2], (N_ROW, N_COL, 2, TC // B, B, B), B ** -0.5, 0.25, ((0, 32), (1, 8)), jnp.float32)
    left_owner = with_ends(jax.random.randint(splits[3], (N_ROW, 2), 0, N_COL), jax.random.fold_in(splits[3], 1), 0, N_COL - 1).astype(jnp.int32)
    right_owner = with_ends(jax.random.randint(splits[4], (N_COL, 2), 0, N_ROW), jax.random.fold_in(splits[4], 1), 0, N_ROW - 1).astype(jnp.int32)
    return {"window": window, "left_slots": left_slots, "right_slots": right_slots, "left_owner": left_owner, "right_owner": right_owner}


full_precision = lax.Precision.HIGHEST


def left_section(matrix, factors):
    block_count = factors.shape[0]
    blocks = matrix.reshape(block_count, factors.shape[1], matrix.shape[1])
    result = jnp.einsum("mkr,mkc->mrc", factors, blocks, precision=full_precision)
    return result.reshape(matrix.shape)


def right_section(matrix, factors):
    block_count = factors.shape[0]
    blocks = matrix.reshape(matrix.shape[0], block_count, factors.shape[1])
    result = jnp.einsum("rmk,mkc->rmc", blocks, factors, precision=full_precision)
    return result.reshape(matrix.shape)


def reference(window, left_slots, right_slots, left_owner, right_owner):
    factor_order = left_slots.shape[-1]
    half_order = factor_order // 2
    rows_total, cols_total = window.shape
    row_ids = jnp.arange(left_owner.shape[0], dtype=jnp.int32)
    col_ids = jnp.arange(right_owner.shape[0], dtype=jnp.int32)
    first_left = left_slots[row_ids, left_owner[:, 0], 0].reshape(-1, factor_order, factor_order)
    second_left = left_slots[row_ids, left_owner[:, 1], 1].reshape(-1, factor_order, factor_order)
    first_right = right_slots[right_owner[:, 0], col_ids, 0].reshape(-1, factor_order, factor_order)
    second_right = right_slots[right_owner[:, 1], col_ids, 1].reshape(-1, factor_order, factor_order)
    current = left_section(window, first_left)
    inside = left_section(current[half_order:rows_total - half_order], second_left[:-1])
    current = jnp.concatenate([current[:half_order], inside, current[rows_total - half_order:]], 0)
    current = right_section(current, first_right)
    inside = right_section(current[:, half_order:cols_total - half_order], second_right[:-1])
    current = jnp.concatenate([current[:, :half_order], inside, current[:, cols_total - half_order:]], 1)
    return current
```

```python
import jax
import jax.numpy as jnp
from jax import lax
from jax.experimental import pallas as pl
from jax.experimental.pallas import tpu as pltpu
from jax.sharding import PartitionSpec as P

MESH = pl.DeviceIdType.MESH
F32, BF16 = jnp.float32, jnp.bfloat16
COPIES = 112
PIECE, HALF = 128, 64


def split(value):
    high = value.astype(BF16)
    return high, (value - high.astype(F32)).astype(BF16)


def product(a, b, contract_a=1):
    dims = (((contract_a,), (0,)), ((), ()))

    def dot(p, q):
        return lax.dot_general(p, q, dims, preferred_element_type=F32)

    return dot(a[0], b[0]) + (dot(a[0], b[1]) + dot(a[1], b[0]))


def kernel(
    left_owner, right_owner, window, left, right, out,
    win, left_own, right_own, right_swap, right_pick,
    first_left, second_left, first_right, second_right,
    arrive, merged, home, left_z, right_z, relay, aside,
    win_split, fl_split, sl_split, fr_split, sr_split,
    mid_split, cur, cur_split, above, below, nxt, nxt_split, from_left, from_right,
    result, send_sem, recv_sem, local_sem,
):
    row, col = lax.axis_index("row"), lax.axis_index("col")
    zh, y, core = row // 8, (row // 2) % 4, row % 2
    zl, x = col // 4, col % 4

    def turn(v, d, n=4):
        return lax.rem(v + d + n, n)

    xp, xm = (row, zl * 4 + turn(x, 1)), (row, zl * 4 + turn(x, -1))
    zpair = (row, (1 - zl) * 4 + x)
    yp, ym = (zh * 8 + turn(y, 1) * 2 + core, col), (zh * 8 + turn(y, -1) * 2 + core, col)
    zp, zm = (turn(zh, 1) * 8 + y * 2 + core, col), (turn(zh, -1) * 8 + y * 2 + core, col)
    mate = (zh * 8 + y * 2 + 1 - core, col)
    row_next, row_prev = (turn(row, 1, 32), col), (turn(row, -1, 32), col)
    col_next, col_prev = (row, turn(col, 1, 8)), (row, turn(col, -1, 8))

    loads = []

    def load(src, dst):
        copy = pltpu.make_async_copy(src, dst, local_sem.at[len(loads)])
        copy.start()
        loads.append(copy)
        return copy

    load_left = [load(left.at[0, 0, s, 0], left_own.at[s]) for s in range(2)]
    load_right = [load(right.at[0, 0, s, core], right_own.at[s]) for s in range(2)]
    load_win = load(window, win)

    partners = (xp, xm, zpair, yp, ym, zp, zm, mate, row_next, row_prev, col_next, col_prev)
    barrier = pltpu.get_barrier_semaphore()
    for partner in partners:
        pl.semaphore_signal(barrier, inc=1, device_id=partner, device_id_type=MESH)
    pl.semaphore_wait(barrier, len(partners))

    made = [0]
    sent = []

    def describe(src, dst, device):
        k = made[0]
        made[0] += 1
        return pltpu.make_async_remote_copy(
            src_ref=src, dst_ref=dst, send_sem=send_sem.at[k], recv_sem=recv_sem.at[k],
            device_id=device, device_id_type=MESH,
        )

    def send(src, dst, device):
        copy = describe(src, dst, device)
        copy.start()
        sent.append(copy)
        return copy

    def rows(piece, part=None):
        if part is None:
            return pl.ds(pl.multiple_of(piece * PIECE, PIECE), PIECE)
        return pl.ds(pl.multiple_of(piece * PIECE + part * HALF, HALF), HALF)

    def scatter_start(ref, pos, plus, minus, f):
        far, ahead, behind = turn(pos, 2), turn(pos, 1), turn(pos, -1)
        return (
            send(ref.at[rows(far, 0)], arrive.at[f, 0], plus),
            send(ref.at[rows(far, 1)], arrive.at[f, 1], minus),
            send(ref.at[rows(ahead, 1)], arrive.at[f, 2], plus),
            send(ref.at[rows(behind, 0)], arrive.at[f, 3], minus),
        )

    def scatter_merge(ref, pos, plus, minus, f, owner, copies):
        ahead, behind = turn(pos, 1), turn(pos, -1)
        copies[0].wait_recv()
        merged[f, 0] = jnp.where(owner == behind, arrive[f, 0], ref[rows(ahead, 0), :])
        one = send(merged.at[f, 0], arrive.at[f, 4], plus)
        copies[1].wait_recv()
        merged[f, 1] = jnp.where(owner == ahead, arrive[f, 1], ref[rows(behind, 1), :])
        two = send(merged.at[f, 1], arrive.at[f, 5], minus)
        return copies + (one, two)

    def scatter_end(ref, pos, f, owner, copies):
        ahead, behind = turn(pos, 1), turn(pos, -1)
        for copy in copies[2:]:
            copy.wait_recv()
        low = jnp.where(owner == ahead, arrive[f, 3], arrive[f, 4])
        home[f, :HALF] = jnp.where(owner == pos, ref[rows(pos, 0), :], low)
        high = jnp.where(owner == behind, arrive[f, 2], arrive[f, 5])
        home[f, HALF:] = jnp.where(owner == pos, ref[rows(pos, 1), :], high)

    def gather_start(ref, pos, plus, minus):
        own = ref.at[rows(pos)]
        return (send(own, own, plus), send(own, own, minus))

    def gather_pass(ref, pos, plus, minus, copies):
        ahead, behind = turn(pos, 1), turn(pos, -1)
        copies[0].wait_recv()
        low = ref.at[rows(behind, 0)]
        one = send(low, low, plus)
        copies[1].wait_recv()
        high = ref.at[rows(ahead, 1)]
        return (one, send(high, high, minus))

    def to_mate(ref, where):
        part = ref.at[where]
        return send(part, part, mate)

    swaps = [[], []]

    def swap(s):
        for d in (2, 1, 3, 0):
            where = rows(turn(y, d))
            swaps[s].append(
                send(right.at[0, 0, s, 1 - core, where], right_swap.at[s, where], mate)
            )

    def pick(s, k, own_core):
        where = rows(turn(y, (2, 1, 3, 0)[k]))
        swaps[s][k].wait_recv()
        right_pick[s, where, :] = jnp.where(
            own_core == core, right_own[s, where, :], right_swap[s, where, :]
        )

    lown = [left_owner[0, s] for s in range(2)]
    rown = [right_owner[0, s] for s in range(2)]
    lx, lz = [v % 4 for v in lown], [v // 4 for v in lown]
    ry, rc, rz = [(v // 2) % 4 for v in rown], [v % 2 for v in rown], [v // 8 for v in rown]

    lscatter, rscatter = [None, None], [None, None]
    lsrc = [left.at[0, 0, s, 0] for s in range(2)]
    lval = [left_own.at[s] for s in range(2)]
    rval = [right_pick.at[s] for s in range(2)]

    def left_start(s):
        lscatter[s] = scatter_start(lsrc[s], x, xp, xm, s)

    def left_merge(s):
        load_left[s].wait()
        lscatter[s] = scatter_merge(lval[s], x, xp, xm, s, lx[s], lscatter[s])

    def left_home(s):
        scatter_end(lval[s], x, s, lx[s], lscatter[s])
        return send(home.at[s], left_z.at[s], zpair)

    def right_start(s):
        load_right[s].wait()
        for k in range(3):
            pick(s, k, rc[s])
        rscatter[s] = scatter_start(rval[s], y, yp, ym, 2 + s)
        pick(s, 3, rc[s])

    def right_merge(s):
        rscatter[s] = scatter_merge(rval[s], y, yp, ym, 2 + s, ry[s], rscatter[s])

    def right_home(s):
        scatter_end(rval[s], y, 2 + s, ry[s], rscatter[s])
        return (
            send(home.at[2 + s, pl.ds(0, HALF)], right_z.at[s, 0], zp),
            send(home.at[2 + s, pl.ds(HALF, HALF)], right_z.at[s, 1], zm),
        )

    def right_relay(s, copies):
        copies[0].wait_recv()
        relay[s, 0] = jnp.where(rz[s] == zh, home[2 + s, HALF:], right_z[s, 0])
        one = send(relay.at[s, 0], right_z.at[s, 2], zp)
        copies[1].wait_recv()
        relay[s, 1] = jnp.where(rz[s] == zh, home[2 + s, :HALF], right_z[s, 1])
        return (one, send(relay.at[s, 1], right_z.at[s, 3], zm))

    def right_piece(s, copies):
        for copy in copies:
            copy.wait_recv()
        own, behind, ahead = rz[s] == zh, rz[s] == turn(zh, -1), rz[s] == turn(zh, 1)
        plus_one, minus_one, plus_two, minus_two = (right_z[s, k] for k in range(4))
        low = jnp.where(behind, plus_one, jnp.where(ahead, minus_two, plus_two))
        high = jnp.where(behind, plus_two, jnp.where(ahead, minus_one, minus_two))
        return jnp.where(own, home[2 + s, :HALF], low), jnp.where(own, home[2 + s, HALF:], high)

    def store_split(pair, where, value):
        high, low = split(value)
        pair[(0, *where)] = high
        pair[(1, *where)] = low

    swap(0)
    left_start(0)
    right_start(0)
    swap(1)
    left_merge(0)
    left_start(1)
    right_merge(0)
    load_win.wait()
    store_split(win_split, (slice(None), slice(None)), win[...])
    right_start(1)
    lz1 = left_home(0)
    left_merge(1)
    rz1 = right_home(0)
    right_merge(1)
    lz1.wait_recv()
    first_left[rows(x), :] = jnp.where(lz[0] == zl, home[0], left_z[0])
    lg1 = gather_start(first_left, x, xp, xm)
    rz1 = right_relay(0, rz1)
    lz2 = left_home(1)
    rz2 = right_home(1)
    lf1 = gather_pass(first_left, x, xp, xm, lg1)
    low, high = right_piece(0, rz1)
    mine = first_right.at[core]
    mine[rows(y, 0), :] = low
    mine[rows(y, 1), :] = high
    rg1 = gather_start(mine, y, yp, ym)
    mates1 = [to_mate(mine, rows(y))]
    lz2.wait_recv()
    piece = jnp.where(lz[1] == zl, home[1], left_z[1])
    second_left[rows(x), :256] = piece[:, :256]
    aside[0] = piece[:, 256:]
    shift_left = send(aside.at[0], second_left.at[rows(x), pl.ds(256, 256)], row_next)
    rz2 = right_relay(1, rz2)
    for copy in lf1:
        copy.wait_recv()
    store_split(fl_split, (slice(None), slice(None)), first_left[...])
    shift_left.wait_recv()
    lg2 = gather_start(second_left, x, xp, xm)
    rf1 = gather_pass(mine, y, yp, ym, rg1)
    mates1 += [to_mate(mine, rows(turn(y, -1))), to_mate(mine, rows(turn(y, 1)))]
    for t in range(4):
        cols = slice(t * 256, t * 256 + 256)
        store_split(
            mid_split,
            (slice(None), cols),
            product((fl_split[0], fl_split[1]), (win_split[0, :, cols], win_split[1, :, cols]), 0),
        )
    low, high = right_piece(1, rz2)
    mine2 = second_right.at[core]
    mine2[rows(y, 0), :256] = low[:, :256]
    mine2[rows(y, 1), :256] = high[:, :256]
    aside[1, :HALF] = low[:, 256:]
    aside[1, HALF:] = high[:, 256:]
    shift_right = describe(aside.at[1], second_right.at[1, rows(y), pl.ds(256, 256)], col_next)

    @pl.when(core == 1)
    def _():
        shift_right.start()

    @pl.when(core == 0)
    def _():
        mine2[rows(y), 256:] = aside[1]

    for copy in rf1:
        copy.wait_recv()
    mates1 += [to_mate(mine, rows(turn(y, 2)))]
    lf2 = gather_pass(second_left, x, xp, xm, lg2)

    @pl.when(core == 1)
    def _():
        shift_right.wait_recv()

    rg2 = gather_start(mine2, y, yp, ym)
    mates2 = [to_mate(mine2, rows(y))]
    for copy in mates1:
        copy.wait_recv()
    for m in range(2):
        store_split(fr_split, (m,), first_right[m])

    order = (0, 3, 1, 2)
    row_swaps = [None] * 4
    for t in order:
        m, h = t // 2, t % 2
        cols, band, part = slice(t * 256, t * 256 + 256), slice(m * 512, m * 512 + 512), slice(h * 256, h * 256 + 256)
        value = product(
            (mid_split[0, :, band], mid_split[1, :, band]),
            (fr_split[0, m, :, part], fr_split[1, m, :, part]),
        )
        cur[t] = value
        store_split(cur_split, (t,), value)
        row_swaps[t] = (
            send(cur.at[t, pl.ds(0, 256)], below.at[t], row_prev),
            send(cur.at[t, pl.ds(256, 256)], above.at[t], row_next),
        )
    rf2 = gather_pass(mine2, y, yp, ym, rg2)
    mates2 += [to_mate(mine2, rows(turn(y, -1))), to_mate(mine2, rows(turn(y, 1)))]
    for copy in lf2:
        copy.wait_recv()
    store_split(sl_split, (slice(None), slice(None)), second_left[...])

    top_stays, bottom_stays = row == 0, row == 31
    col_swaps = []
    for t in order:
        for copy in row_swaps[t]:
            copy.wait_recv()
        up, down = split(above[t]), split(below[t])
        top = (cur_split[0, t, :256], cur_split[1, t, :256])
        bottom = (cur_split[0, t, 256:], cur_split[1, t, 256:])

        def factor(k, side):
            at = (slice(k * 256, k * 256 + 256), slice(side * 256, side * 256 + 256))
            return sl_split[(0, *at)], sl_split[(1, *at)]

        new_top = product(factor(0, 1), up, 0) + product(factor(1, 1), top, 0)
        new_bottom = product(factor(0, 0), bottom, 0) + product(factor(1, 0), down, 0)
        new_top = jnp.where(top_stays, cur[t, :256], new_top)
        new_bottom = jnp.where(bottom_stays, cur[t, 256:], new_bottom)
        nxt[t, :256] = new_top
        nxt[t, 256:] = new_bottom
        store_split(nxt_split, (t, slice(0, 256)), new_top)
        store_split(nxt_split, (t, slice(256, 512)), new_bottom)
        if t == 0:
            col_swaps.append(send(nxt.at[0], from_right, col_prev))
        if t == 3:
            col_swaps.append(send(nxt.at[3], from_left, col_next))
        if t == 3:
            for copy in rf2:
                copy.wait_recv()
            mates2 += [to_mate(mine2, rows(turn(y, 2)))]
    for copy in mates2:
        copy.wait_recv()
    for m in range(2):
        store_split(sr_split, (m,), second_right[m])

    def step(t, m, k, side):
        at = (m, slice(k * 256, k * 256 + 256), slice(side * 256, side * 256 + 256))
        return product((nxt_split[0, t], nxt_split[1, t]), (sr_split[(0, *at)], sr_split[(1, *at)]))

    for side in range(2):
        result[:, 256 + side * 256 : 512 + side * 256] = step(1, 0, 0, side) + step(2, 0, 1, side)
    col_swaps[0].wait_recv()
    other = split(from_right[...])
    edge = step(3, 1, 0, 0) + product(other, (sr_split[0, 1, 256:, :256], sr_split[1, 1, 256:, :256]))
    result[:, 768:] = jnp.where(col == 7, nxt[3], edge)
    col_swaps[1].wait_recv()
    other = split(from_left[...])
    edge = step(0, 1, 1, 1) + product(other, (sr_split[0, 1, :256, 256:], sr_split[1, 1, :256, 256:]))
    result[:, :256] = jnp.where(col == 0, nxt[0], edge)
    store = pltpu.make_async_copy(result, out, local_sem.at[len(loads)])
    store.start()
    for copy in sent:
        copy.wait_send()

    @pl.when(core == 1)
    def _():
        shift_right.wait_send()

    store.wait()


def shards(window, left_slots, right_slots, left_owner, right_owner):
    scratch = [
        pltpu.VMEM((512, 1024), F32),
        pltpu.VMEM((2, 512, 512), F32),
        pltpu.VMEM((2, 512, 512), F32),
        pltpu.VMEM((2, 512, 512), F32),
        pltpu.VMEM((2, 512, 512), F32),
        pltpu.VMEM((512, 512), F32),
        pltpu.VMEM((512, 512), F32),
        pltpu.VMEM((2, 512, 512), F32),
        pltpu.VMEM((2, 512, 512), F32),
        pltpu.VMEM((4, 6, HALF, 512), F32),
        pltpu.VMEM((4, 2, HALF, 512), F32),
        pltpu.VMEM((4, PIECE, 512), F32),
        pltpu.VMEM((2, PIECE, 512), F32),
        pltpu.VMEM((2, 4, HALF, 512), F32),
        pltpu.VMEM((2, 2, HALF, 512), F32),
        pltpu.VMEM((2, PIECE, 256), F32),
        pltpu.VMEM((2, 512, 1024), BF16),
        pltpu.VMEM((2, 512, 512), BF16),
        pltpu.VMEM((2, 512, 512), BF16),
        pltpu.VMEM((2, 2, 512, 512), BF16),
        pltpu.VMEM((2, 2, 512, 512), BF16),
        pltpu.VMEM((2, 512, 1024), BF16),
        pltpu.VMEM((4, 512, 256), F32),
        pltpu.VMEM((2, 4, 512, 256), BF16),
        pltpu.VMEM((4, 256, 256), F32),
        pltpu.VMEM((4, 256, 256), F32),
        pltpu.VMEM((4, 512, 256), F32),
        pltpu.VMEM((2, 4, 512, 256), BF16),
        pltpu.VMEM((512, 256), F32),
        pltpu.VMEM((512, 256), F32),
        pltpu.VMEM((512, 1024), F32),
        pltpu.SemaphoreType.DMA((COPIES,)),
        pltpu.SemaphoreType.DMA((COPIES,)),
        pltpu.SemaphoreType.DMA((8,)),
    ]
    smem, hbm = pl.BlockSpec(memory_space=pltpu.SMEM), pl.BlockSpec(memory_space=pl.ANY)
    return pl.pallas_call(
        kernel,
        name="far_update",
        out_shape=jax.ShapeDtypeStruct(window.shape, F32),
        in_specs=[smem, smem, hbm, hbm, hbm],
        out_specs=hbm,
        scratch_shapes=scratch,
        compiler_params=pltpu.CompilerParams(
            collective_id=0, has_side_effects=True, vmem_limit_bytes=58 * 2**20
        ),
    )(left_owner, right_owner, window, left_slots, right_slots)


def solution(mesh):
    in_specs = (
        P("row", "col"),
        P("row", "col", None, None, None, None),
        P("row", "col", None, None, None, None),
        P("row", None),
        P("col", None),
    )
    out_specs = P("row", "col")
    return jax.shard_map(shards, mesh=mesh, in_specs=in_specs, out_specs=out_specs, check_vma=False)
```

```python
import functools

import jax
import jax.numpy as jnp
from jax import lax
from jax.experimental import pallas as pl
from jax.experimental.pallas import tpu as pltpu
from jax.sharding import PartitionSpec as P

MESH = pl.DeviceIdType.MESH
F32, BF16 = jnp.float32, jnp.bfloat16
COPIES = 176
PIECE, HALF = 128, 64
ORDER = (
    "L1a.start", "R1a.swap", "win", "R1b.swap", "R2a.swap", "L1b.start", "R1a.start", "L1a.merge",
    "R1b.start", "L1b.merge", "L1a.home", "L2b.start", "R1a.merge", "L1b.home", "R1b.merge", "R2b.swap",
    "L2a.start", "R1a.home", "R1b.home", "R2a.start", "L2b.merge", "R2b.start", "L1a.piece", "L2b.home",
    "L1b.piece", "R1b.relay", "R2a.merge", "L2a.merge", "R2b.merge", "L1b.pass", "L1a.pass", "R1a.relay",
    "L2b.shift", "R1b.piece", "L2a.home", "L2b.piece", "R2b.home", "R1a.piece", "L1b.done", "R1b.pass",
    "L1a.done", "x1.0", "L2a.piece", "x1.1", "x1.2", "L2a.pass", "R2b.relay", "L2b.pass", "R1a.pass",
    "R1b.last", "hop0", "x1.3", "hop1", "hop2", "R2a.home", "L2a.done", "L2b.done", "R1b.done", "x2.0",
    "R2b.shift", "hop3", "x2.1", "R1a.last", "R2a.relay", "x2.2", "R2b.piece", "R1a.done", "x2.3", "x3.0",
    "R2a.piece", "x3.3", "x3.2", "x3.1", "R2b.pass", "R2a.pass", "R2b.last", "R2a.last", "R2b.done",
    "R2a.done", "mid", "edgeR", "edgeL",
)


def split(value):
    high = value.astype(BF16)
    return high, (value - high.astype(F32)).astype(BF16)


def product(a, b, contract_a=1):
    dims = (((contract_a,), (0,)), ((), ()))

    def dot(p, q):
        return lax.dot_general(p, q, dims, preferred_element_type=F32)

    return dot(a[0], b[0]) + (dot(a[0], b[1]) + dot(a[1], b[0]))


def kernel(
    left_owner, right_owner, window, left, right, out,
    win, left_own, right_own, right_swap, right_pick,
    first_left, second_left, first_right, second_right,
    arrive, merged, home, left_z, right_z, relay, aside,
    win_split, fl_split, sl_split, fr_split, sr_split,
    mid_split, cur, cur_split, above, below, hop, nxt, nxt_split, from_left, from_right,
    result, send_sem, recv_sem, local_sem,
):
    row, col = lax.axis_index("row"), lax.axis_index("col")
    zh, y, core = row // 8, (row // 2) % 4, row % 2
    zl, x = col // 4, col % 4

    def turn(v, d, n=4):
        return lax.rem(v + d + n, n)

    xp, xm = (row, zl * 4 + turn(x, 1)), (row, zl * 4 + turn(x, -1))
    zpair = (row, (1 - zl) * 4 + x)
    yp, ym = (zh * 8 + turn(y, 1) * 2 + core, col), (zh * 8 + turn(y, -1) * 2 + core, col)
    zp, zm = (turn(zh, 1) * 8 + y * 2 + core, col), (turn(zh, -1) * 8 + y * 2 + core, col)
    mate = (zh * 8 + y * 2 + 1 - core, col)
    row_next, row_prev = (turn(row, 1, 32), col), (turn(row, -1, 32), col)
    col_next, col_prev = (row, turn(col, 1, 8)), (row, turn(col, -1, 8))

    loads = []

    def load(src, dst):
        copy = pltpu.make_async_copy(src, dst, local_sem.at[len(loads)])
        copy.start()
        loads.append(copy)
        return copy

    load_left = [load(left.at[0, 0, s, 0], left_own.at[s]) for s in range(2)]
    load_right = [load(right.at[0, 0, s, core], right_own.at[s]) for s in range(2)]
    load_win = load(window, win)
    loaded = []

    def need(copy):
        if not any(copy is other for other in loaded):
            copy.wait()
            loaded.append(copy)

    is_last, is_first = (y == 3) & (core == 1), (y == 0) & (core == 0)
    across = (zh * 8 + 7 - y * 2 - core, col)
    partners = (
        xp, xm, zpair, yp, ym, zp, zm, mate, row_next, row_prev, col_next, col_prev, across,
    )
    barrier = pltpu.get_barrier_semaphore()
    for partner in partners:
        pl.semaphore_signal(barrier, inc=1, device_id=partner, device_id_type=MESH)
    pl.semaphore_wait(barrier, len(partners))

    made = [0]
    sent = []

    def describe(src, dst, device):
        k = made[0]
        made[0] += 1
        return pltpu.make_async_remote_copy(
            src_ref=src, dst_ref=dst, send_sem=send_sem.at[k], recv_sem=recv_sem.at[k],
            device_id=device, device_id_type=MESH,
        )

    def send(src, dst, device):
        copy = describe(src, dst, device)
        copy.start()
        sent.append(copy)
        return copy

    def rows(piece, part=None):
        if part is None:
            return pl.ds(pl.multiple_of(piece * PIECE, PIECE), PIECE)
        return pl.ds(pl.multiple_of(piece * PIECE + part * HALF, HALF), HALF)

    def scatter_start(ref, pos, plus, minus, f):
        far, ahead, behind = turn(pos, 2), turn(pos, 1), turn(pos, -1)
        return (
            send(ref(rows(far, 0)), arrive.at[f, 0], plus),
            send(ref(rows(far, 1)), arrive.at[f, 1], minus),
            send(ref(rows(ahead, 1)), arrive.at[f, 2], plus),
            send(ref(rows(behind, 0)), arrive.at[f, 3], minus),
        )

    def scatter_merge(value, pos, plus, minus, f, owner, copies):
        ahead, behind = turn(pos, 1), turn(pos, -1)
        copies[0].wait_recv()
        merged[f, 0] = jnp.where(owner == behind, arrive[f, 0], value(rows(ahead, 0)))
        one = send(merged.at[f, 0], arrive.at[f, 4], plus)
        copies[1].wait_recv()
        merged[f, 1] = jnp.where(owner == ahead, arrive[f, 1], value(rows(behind, 1)))
        two = send(merged.at[f, 1], arrive.at[f, 5], minus)
        return copies + (one, two)

    def scatter_end(value, pos, f, owner, copies):
        ahead, behind = turn(pos, 1), turn(pos, -1)
        for copy in copies[2:]:
            copy.wait_recv()
        low = jnp.where(owner == ahead, arrive[f, 3], arrive[f, 4])
        home[f, :HALF] = jnp.where(owner == pos, value(rows(pos, 0)), low)
        high = jnp.where(owner == behind, arrive[f, 2], arrive[f, 5])
        home[f, HALF:] = jnp.where(owner == pos, value(rows(pos, 1)), high)

    def gather_start(ref, pos, plus, minus):
        own = ref.at[rows(pos)]
        return (send(own, own, plus), send(own, own, minus))

    def gather_pass(ref, pos, plus, minus, copies):
        ahead, behind = turn(pos, 1), turn(pos, -1)
        copies[0].wait_recv()
        low = ref.at[rows(behind, 0)]
        one = send(low, low, plus)
        copies[1].wait_recv()
        high = ref.at[rows(ahead, 1)]
        return (one, send(high, high, minus))

    def to_mate(ref, where):
        part = ref.at[where]
        return send(part, part, mate)

    def store_split(pair, where, value):
        high, low = split(value)
        pair[(0, *where)] = high
        pair[(1, *where)] = low

    lown = [left_owner[0, s] for s in range(2)]
    rown = [right_owner[0, s] for s in range(2)]
    lx, lz = [v % 4 for v in lown], [v // 4 for v in lown]
    ry, rc, rz = [(v // 2) % 4 for v in rown], [v % 2 for v in rown], [v // 8 for v in rown]
    steps = {}
    at = {}

    def left_unit(s, h, name):
        f, here = s * 2 + h, pl.ds(h * 256, 256)
        place = (first_left, second_left)[s].at[h]
        pair = (fl_split, sl_split)[s]

        def ref(where):
            return left.at[0, 0, s, 0, where, here]

        def value(where):
            return left_own[s, where, here]

        def start():
            at[f] = scatter_start(ref, x, xp, xm, f)

        def merge():
            need(load_left[s])
            at[f] = scatter_merge(value, x, xp, xm, f, lx[s], at[f])

        def end():
            scatter_end(value, x, f, lx[s], at[f])
            at[f] = send(home.at[f], left_z.at[f], zpair)

        def chosen():
            at[f].wait_recv()
            return jnp.where(lz[s] == zl, home[f], left_z[f])

        def shift():
            aside[0] = chosen()
            at[f] = send(aside.at[0], place.at[rows(x)], row_next)

        def piece():
            if (s, h) == (1, 1):
                at[f].wait_recv()
            else:
                place[rows(x), :] = chosen()
            at[f] = gather_start(place, x, xp, xm)

        def forward():
            at[f] = gather_pass(place, x, xp, xm, at[f])

        def done():
            for copy in at[f]:
                copy.wait_recv()
            store_split(pair, (h,), place[...])

        steps.update({
            name + ".start": start, name + ".merge": merge, name + ".home": end, name + ".shift": shift,
            name + ".piece": piece, name + ".pass": forward, name + ".done": done,
        })

    def right_unit(s, h, name):
        f, g, here = 4 + s * 2 + h, s * 2 + h, pl.ds(h * 256, 256)
        both = (first_right, second_right)[s]
        place = both.at[core, h]
        pair = (fr_split, sr_split)[s]
        mates = []

        def ref(where):
            return right_pick.at[g, where]

        def value(where):
            return right_pick[g, where, :]

        def swap():
            at[f] = send(right.at[0, 0, s, 1 - core, :, here], right_swap.at[g], mate)

        def start():
            need(load_right[s])
            at[f].wait_recv()
            right_pick[g] = jnp.where(rc[s] == core, right_own[s, :, here], right_swap[g])
            at[f] = scatter_start(ref, y, yp, ym, f)

        def merge():
            at[f] = scatter_merge(value, y, yp, ym, f, ry[s], at[f])

        def end():
            scatter_end(value, y, f, ry[s], at[f])
            at[f] = (
                send(home.at[f, pl.ds(0, HALF)], right_z.at[g, 0], zp),
                send(home.at[f, pl.ds(HALF, HALF)], right_z.at[g, 1], zm),
            )

        def pass_on():
            one, two = at[f]
            one.wait_recv()
            relay[g, 0] = jnp.where(rz[s] == zh, home[f, HALF:], right_z[g, 0])
            three = send(relay.at[g, 0], right_z.at[g, 2], zp)
            two.wait_recv()
            relay[g, 1] = jnp.where(rz[s] == zh, home[f, :HALF], right_z[g, 1])
            at[f] = (three, send(relay.at[g, 1], right_z.at[g, 3], zm))

        def chosen():
            for copy in at[f]:
                copy.wait_recv()
            own, behind, ahead = rz[s] == zh, rz[s] == turn(zh, -1), rz[s] == turn(zh, 1)
            plus_one, minus_one, plus_two, minus_two = (right_z[g, k] for k in range(4))
            low = jnp.where(behind, plus_one, jnp.where(ahead, minus_two, plus_two))
            high = jnp.where(behind, plus_two, jnp.where(ahead, minus_one, minus_two))
            return jnp.where(own, home[f, :HALF], low), jnp.where(own, home[f, HALF:], high)

        def shift():
            aside[1, :HALF], aside[1, HALF:] = chosen()
            at[f] = describe(aside.at[1], second_right.at[1, 1, rows(y)], col_next)
            at["shift"] = at[f]

            @pl.when(core == 1)
            def _():
                at[f].start()

            @pl.when(core == 0)
            def _():
                place[rows(y), :] = aside[1]

        def piece():
            if (s, h) == (1, 1):

                @pl.when(core == 1)
                def _():
                    at[f].wait_recv()
            else:
                place[rows(y, 0), :], place[rows(y, 1), :] = chosen()
            at[f] = gather_start(place, y, yp, ym)
            mates.append(to_mate(place, rows(y)))

        def forward():
            at[f] = gather_pass(place, y, yp, ym, at[f])
            mates.append(to_mate(place, rows(turn(y, -1))))
            mates.append(to_mate(place, rows(turn(y, 1))))

        def last():
            for copy in at[f]:
                copy.wait_recv()
            mates.append(to_mate(place, rows(turn(y, 2))))

        def done():
            for copy in mates:
                copy.wait_recv()
            for m in range(2):
                store_split(pair, (m, h), both[m, h])

        steps.update({
            name + ".swap": swap, name + ".start": start, name + ".merge": merge, name + ".home": end,
            name + ".relay": pass_on, name + ".shift": shift, name + ".piece": piece, name + ".pass": forward,
            name + ".last": last, name + ".done": done,
        })

    for s in range(2):
        for h in range(2):
            tail = "12"[s] + "ab"[h]
            left_unit(s, h, "L" + tail)
            right_unit(s, h, "R" + tail)

    def border_send(t):
        up, down = cur.at[t, pl.ds(0, 256)], cur.at[t, pl.ds(256, 256)]
        to_prev = describe(up, below.at[t], row_prev)
        to_next = describe(down, above.at[t], row_next)
        last = [
            describe(cur.at[t, pl.ds(256, 128)], hop.at[t, 0], zp),
            describe(cur.at[t, pl.ds(384, 128)], hop.at[t, 1], across),
        ]
        first = [
            describe(cur.at[t, pl.ds(0, 128)], hop.at[t, 0], zm),
            describe(cur.at[t, pl.ds(128, 128)], hop.at[t, 1], across),
        ]
        last_on = [
            describe(hop.at[t, 0], above.at[t, pl.ds(0, 128)], across),
            describe(hop.at[t, 1], below.at[t, pl.ds(128, 128)], zm),
        ]
        first_on = [
            describe(hop.at[t, 0], below.at[t, pl.ds(0, 128)], across),
            describe(hop.at[t, 1], above.at[t, pl.ds(128, 128)], zp),
        ]

        @pl.when(~is_last)
        def _():
            to_next.start()

        @pl.when(~is_first)
        def _():
            to_prev.start()

        @pl.when(is_last)
        def _():
            for copy in last:
                copy.start()

        @pl.when(is_first)
        def _():
            for copy in first:
                copy.start()

        return to_prev, to_next, last, first, last_on, first_on

    def border_pass(copies):
        _, _, last, first, last_on, first_on = copies

        @pl.when(is_last)
        def _():
            last[0].wait_recv()
            last_on[0].start()
            first[1].wait_recv()
            last_on[1].start()

        @pl.when(is_first)
        def _():
            first[0].wait_recv()
            first_on[0].start()
            last[1].wait_recv()
            first_on[1].start()

    def border_wait(copies):
        to_prev, to_next, _, _, last_on, first_on = copies

        @pl.when(~is_last)
        def _():
            to_prev.wait_recv()

        @pl.when(~is_first)
        def _():
            to_next.wait_recv()

        @pl.when(is_last)
        def _():
            first_on[0].wait_recv()
            last_on[1].wait_recv()

        @pl.when(is_first)
        def _():
            last_on[0].wait_recv()
            first_on[1].wait_recv()

    def border_end(copies):
        to_prev, to_next, last, first, last_on, first_on = copies

        @pl.when(~is_last)
        def _():
            to_next.wait_send()

        @pl.when(~is_first)
        def _():
            to_prev.wait_send()

        @pl.when(is_last)
        def _():
            for copy in last + last_on:
                copy.wait_send()

        @pl.when(is_first)
        def _():
            for copy in first + first_on:
                copy.wait_send()

    top_stays, bottom_stays = row == 0, row == 31
    row_swaps, col_swaps = {}, {}

    def win_step():
        need(load_win)
        store_split(win_split, (slice(None), slice(None)), win[...])

    def first_rows(t):
        cols = slice(t * 256, t * 256 + 256)
        for h in range(2):
            part = slice(h * 256, h * 256 + 256)
            value = product(
                (fl_split[0, h], fl_split[1, h]), (win_split[0, :, cols], win_split[1, :, cols]), 0
            )
            cur[t, part] = value
            store_split(cur_split, (t, part), value)
        row_swaps[t] = border_send(t)

    def second_rows(t):
        border_wait(row_swaps[t])
        cols = slice(t * 256, t * 256 + 256)
        top = (cur_split[0, t, :256], cur_split[1, t, :256])
        bottom = (cur_split[0, t, 256:], cur_split[1, t, 256:])

        def blend(h, upper, lower):
            one = product((sl_split[0, h, :256], sl_split[1, h, :256]), upper, 0)
            return one + product((sl_split[0, h, 256:], sl_split[1, h, 256:]), lower, 0)

        new_bottom = blend(0, bottom, split(below[t]))
        new_top = blend(1, split(above[t]), top)
        new_top = jnp.where(top_stays, cur[t, :256], new_top)
        new_bottom = jnp.where(bottom_stays, cur[t, 256:], new_bottom)
        store_split(mid_split, (slice(0, 256), cols), new_top)
        store_split(mid_split, (slice(256, 512), cols), new_bottom)

    def first_cols(t):
        m, h = t // 2, t % 2
        band = slice(m * 512, m * 512 + 512)
        value = product(
            (mid_split[0, :, band], mid_split[1, :, band]), (fr_split[0, m, h], fr_split[1, m, h])
        )
        nxt[t] = value
        store_split(nxt_split, (t,), value)
        if t == 0:
            col_swaps[t] = send(nxt.at[0], from_right, col_prev)
        if t == 3:
            col_swaps[t] = send(nxt.at[3], from_left, col_next)

    def term(value, m, h, k):
        part = slice(k * 256, k * 256 + 256)
        return product(value, (sr_split[0, m, h, part], sr_split[1, m, h, part]))

    def kept(t):
        return nxt_split[0, t], nxt_split[1, t]

    def middle():
        for h in range(2):
            result[:, 256 + h * 256 : 512 + h * 256] = term(kept(1), 0, h, 0) + term(kept(2), 0, h, 1)

    def right_edge():
        edge = term(kept(3), 1, 0, 0)
        col_swaps[0].wait_recv()
        edge = edge + term(split(from_right[...]), 1, 0, 1)
        result[:, 768:] = jnp.where(col == 7, nxt[3], edge)

    def left_edge():
        edge = term(kept(0), 1, 1, 1)
        col_swaps[3].wait_recv()
        edge = edge + term(split(from_left[...]), 1, 1, 0)
        result[:, :256] = jnp.where(col == 0, nxt[0], edge)

    steps.update({"win": win_step, "mid": middle, "edgeR": right_edge, "edgeL": left_edge})
    for t in range(4):
        steps.update({
            "x1." + str(t): functools.partial(first_rows, t), "x2." + str(t): functools.partial(second_rows, t),
            "x3." + str(t): functools.partial(first_cols, t),
            "hop" + str(t): lambda t=t: border_pass(row_swaps[t]),
        })
    for name in ORDER:
        steps[name]()
    store = pltpu.make_async_copy(result, out, local_sem.at[len(loads)])
    store.start()
    for copy in sent:
        copy.wait_send()
    for copies in row_swaps.values():
        border_end(copies)

    @pl.when(core == 1)
    def _():
        at["shift"].wait_send()

    store.wait()


def shards(window, left_slots, right_slots, left_owner, right_owner):
    scratch = [
        pltpu.VMEM((512, 1024), F32),
        pltpu.VMEM((2, 512, 512), F32),
        pltpu.VMEM((2, 512, 512), F32),
        pltpu.VMEM((4, 512, 256), F32),
        pltpu.VMEM((4, 512, 256), F32),
        pltpu.VMEM((2, 512, 256), F32),
        pltpu.VMEM((2, 512, 256), F32),
        pltpu.VMEM((2, 2, 512, 256), F32),
        pltpu.VMEM((2, 2, 512, 256), F32),
        pltpu.VMEM((8, 6, HALF, 256), F32),
        pltpu.VMEM((8, 2, HALF, 256), F32),
        pltpu.VMEM((8, PIECE, 256), F32),
        pltpu.VMEM((4, PIECE, 256), F32),
        pltpu.VMEM((4, 4, HALF, 256), F32),
        pltpu.VMEM((4, 2, HALF, 256), F32),
        pltpu.VMEM((2, PIECE, 256), F32),
        pltpu.VMEM((2, 512, 1024), BF16),
        pltpu.VMEM((2, 2, 512, 256), BF16),
        pltpu.VMEM((2, 2, 512, 256), BF16),
        pltpu.VMEM((2, 2, 2, 512, 256), BF16),
        pltpu.VMEM((2, 2, 2, 512, 256), BF16),
        pltpu.VMEM((2, 512, 1024), BF16),
        pltpu.VMEM((4, 512, 256), F32),
        pltpu.VMEM((2, 4, 512, 256), BF16),
        pltpu.VMEM((4, 256, 256), F32),
        pltpu.VMEM((4, 256, 256), F32),
        pltpu.VMEM((4, 2, 128, 256), F32),
        pltpu.VMEM((4, 512, 256), F32),
        pltpu.VMEM((2, 4, 512, 256), BF16),
        pltpu.VMEM((512, 256), F32),
        pltpu.VMEM((512, 256), F32),
        pltpu.VMEM((512, 1024), F32),
        pltpu.SemaphoreType.DMA((COPIES,)),
        pltpu.SemaphoreType.DMA((COPIES,)),
        pltpu.SemaphoreType.DMA((8,)),
    ]
    smem, hbm = pl.BlockSpec(memory_space=pltpu.SMEM), pl.BlockSpec(memory_space=pl.ANY)
    return pl.pallas_call(
        kernel,
        name="far_update",
        out_shape=jax.ShapeDtypeStruct(window.shape, F32),
        in_specs=[smem, smem, hbm, hbm, hbm],
        out_specs=hbm,
        scratch_shapes=scratch,
        compiler_params=pltpu.CompilerParams(
            collective_id=0, has_side_effects=True, vmem_limit_bytes=58 * 2**20
        ),
    )(left_owner, right_owner, window, left_slots, right_slots)


def solution(mesh):
    in_specs = (
        P("row", "col"),
        P("row", "col", None, None, None, None),
        P("row", "col", None, None, None, None),
        P("row", None),
        P("col", None),
    )
    out_specs = P("row", "col")
    return jax.shard_map(shards, mesh=mesh, in_specs=in_specs, out_specs=out_specs, check_vma=False)
```

```python
import functools

import jax
import jax.numpy as jnp
from jax import lax
from jax.experimental import pallas as pl
from jax.experimental.pallas import tpu as pltpu
from jax.sharding import PartitionSpec as P

MESH = pl.DeviceIdType.MESH
F32, BF16 = jnp.float32, jnp.bfloat16
COPIES = 176
PIECE, HALF = 128, 64
ORDER = (
    "L1b.start", "R1b.swap", "win", "R1a.swap", "R2b.swap", "L1a.start", "R2a.swap", "R1b.start", "L1b.merge",
    "R1a.start", "L1a.merge", "L1b.home", "L2b.start", "R1b.merge", "L1a.home", "R1a.merge", "R2b.start",
    "L2a.start", "R1b.home", "L1b.piece", "R1a.home", "L2b.merge", "R2a.start", "R2b.merge", "R1b.relay",
    "L2a.merge", "L1a.piece", "L1b.pass", "L2b.home", "R2a.merge", "R1a.relay", "R1b.piece", "L1a.pass",
    "L2a.home", "L2b.shift", "R2b.home", "R1a.piece", "R1b.pass", "L1a.done", "L1b.done", "L2b.piece", "x1.0",
    "L2a.piece", "R1b.last", "R2a.home", "x1.1", "hop0", "x1.2", "R1a.pass", "L2b.pass", "R1b.done",
    "L2a.pass", "R2b.relay", "L2b.done", "x1.3", "hop1", "L2a.done", "hop2", "x2.0", "R1a.last", "R2a.relay",
    "R2b.shift", "hop3", "x2.1", "R1a.done", "x3.0", "R2b.piece", "x2.2", "R2a.piece", "x2.3", "x3.3",
    "R2b.pass", "R2a.pass", "R2b.last", "x3.2", "R2a.last", "x3.1", "R2b.done", "R2a.done", "mid", "edgeR",
    "edgeL",
)


def split(value):
    high = value.astype(BF16)
    return high, (value - high.astype(F32)).astype(BF16)


def product(a, b, contract_a=1):
    dims = (((contract_a,), (0,)), ((), ()))

    def dot(p, q):
        return lax.dot_general(p, q, dims, preferred_element_type=F32)

    return dot(a[0], b[0]) + (dot(a[0], b[1]) + dot(a[1], b[0]))


def kernel(
    left_owner, right_owner, window, left, right, out,
    win, left_own, right_own, right_swap, right_pick,
    first_left, second_left, first_right, second_right,
    arrive, merged, home, left_z, right_z, relay, aside,
    win_split, fl_split, sl_split, fr_split, sr_split,
    mid_split, cur, cur_split, above, below, hop, nxt, nxt_split, from_left, from_right,
    result, send_sem, recv_sem, local_sem,
):
    row, col = lax.axis_index("row"), lax.axis_index("col")
    zh, y, core = row // 8, (row // 2) % 4, row % 2
    zl, x = col // 4, col % 4

    def turn(v, d, n=4):
        return lax.rem(v + d + n, n)

    xp, xm = (row, zl * 4 + turn(x, 1)), (row, zl * 4 + turn(x, -1))
    zpair = (row, (1 - zl) * 4 + x)
    yp, ym = (zh * 8 + turn(y, 1) * 2 + core, col), (zh * 8 + turn(y, -1) * 2 + core, col)
    zp, zm = (turn(zh, 1) * 8 + y * 2 + core, col), (turn(zh, -1) * 8 + y * 2 + core, col)
    mate = (zh * 8 + y * 2 + 1 - core, col)
    row_next, row_prev = (turn(row, 1, 32), col), (turn(row, -1, 32), col)
    col_next, col_prev = (row, turn(col, 1, 8)), (row, turn(col, -1, 8))

    loads = []

    def load(src, dst):
        copy = pltpu.make_async_copy(src, dst, local_sem.at[len(loads)])
        copy.start()
        loads.append(copy)
        return copy

    load_left = [load(left.at[0, 0, s, 0], left_own.at[s]) for s in range(2)]
    load_right = [load(right.at[0, 0, s, core], right_own.at[s]) for s in range(2)]
    load_win = load(window, win)
    loaded = []

    def need(copy):
        if not any(copy is other for other in loaded):
            copy.wait()
            loaded.append(copy)

    is_last, is_first = (y == 3) & (core == 1), (y == 0) & (core == 0)
    across = (zh * 8 + 7 - y * 2 - core, col)
    partners = (
        xp, xm, zpair, yp, ym, zp, zm, mate, row_next, row_prev, col_next, col_prev, across,
    )
    barrier = pltpu.get_barrier_semaphore()
    for partner in partners:
        pl.semaphore_signal(barrier, inc=1, device_id=partner, device_id_type=MESH)
    pl.semaphore_wait(barrier, len(partners))

    made = [0]
    sent = []

    def describe(src, dst, device):
        k = made[0]
        made[0] += 1
        return pltpu.make_async_remote_copy(
            src_ref=src, dst_ref=dst, send_sem=send_sem.at[k], recv_sem=recv_sem.at[k],
            device_id=device, device_id_type=MESH,
        )

    def send(src, dst, device):
        copy = describe(src, dst, device)
        copy.start()
        sent.append(copy)
        return copy

    def rows(piece, part=None):
        if part is None:
            return pl.ds(pl.multiple_of(piece * PIECE, PIECE), PIECE)
        return pl.ds(pl.multiple_of(piece * PIECE + part * HALF, HALF), HALF)

    def scatter_start(ref, pos, plus, minus, f):
        far, ahead, behind = turn(pos, 2), turn(pos, 1), turn(pos, -1)
        return (
            send(ref(rows(far, 0)), arrive.at[f, 0], plus),
            send(ref(rows(far, 1)), arrive.at[f, 1], minus),
            send(ref(rows(ahead, 1)), arrive.at[f, 2], plus),
            send(ref(rows(behind, 0)), arrive.at[f, 3], minus),
        )

    def scatter_merge(value, pos, plus, minus, f, owner, copies):
        ahead, behind = turn(pos, 1), turn(pos, -1)
        copies[0].wait_recv()
        merged[f, 0] = jnp.where(owner == behind, arrive[f, 0], value(rows(ahead, 0)))
        one = send(merged.at[f, 0], arrive.at[f, 4], plus)
        copies[1].wait_recv()
        merged[f, 1] = jnp.where(owner == ahead, arrive[f, 1], value(rows(behind, 1)))
        two = send(merged.at[f, 1], arrive.at[f, 5], minus)
        return copies + (one, two)

    def scatter_end(value, pos, f, owner, copies):
        ahead, behind = turn(pos, 1), turn(pos, -1)
        for copy in copies[2:]:
            copy.wait_recv()
        low = jnp.where(owner == ahead, arrive[f, 3], arrive[f, 4])
        home[f, :HALF] = jnp.where(owner == pos, value(rows(pos, 0)), low)
        high = jnp.where(owner == behind, arrive[f, 2], arrive[f, 5])
        home[f, HALF:] = jnp.where(owner == pos, value(rows(pos, 1)), high)

    def gather_start(ref, pos, plus, minus):
        own = ref.at[rows(pos)]
        return (send(own, own, plus), send(own, own, minus))

    def gather_pass(ref, pos, plus, minus, copies):
        ahead, behind = turn(pos, 1), turn(pos, -1)
        copies[0].wait_recv()
        low = ref.at[rows(behind, 0)]
        one = send(low, low, plus)
        copies[1].wait_recv()
        high = ref.at[rows(ahead, 1)]
        return (one, send(high, high, minus))

    def to_mate(ref, where):
        part = ref.at[where]
        return send(part, part, mate)

    def store_split(pair, where, value):
        high, low = split(value)
        pair[(0, *where)] = high
        pair[(1, *where)] = low

    lown = [left_owner[0, s] for s in range(2)]
    rown = [right_owner[0, s] for s in range(2)]
    lx, lz = [v % 4 for v in lown], [v // 4 for v in lown]
    ry, rc, rz = [(v // 2) % 4 for v in rown], [v % 2 for v in rown], [v // 8 for v in rown]
    steps = {}
    at = {}

    def left_unit(s, h, name):
        f, here = s * 2 + h, pl.ds(h * 256, 256)
        place = (first_left, second_left)[s].at[h]
        pair = (fl_split, sl_split)[s]

        def ref(where):
            return left_own.at[s, where, here]

        def value(where):
            return left_own[s, where, here]

        def start():
            need(load_left[s])
            at[f] = scatter_start(ref, x, xp, xm, f)

        def merge():
            need(load_left[s])
            at[f] = scatter_merge(value, x, xp, xm, f, lx[s], at[f])

        def end():
            scatter_end(value, x, f, lx[s], at[f])
            at[f] = send(home.at[f], left_z.at[f], zpair)

        def chosen():
            at[f].wait_recv()
            return jnp.where(lz[s] == zl, home[f], left_z[f])

        def shift():
            aside[0] = chosen()
            at[f] = send(aside.at[0], place.at[rows(x)], row_next)

        def piece():
            if (s, h) == (1, 1):
                at[f].wait_recv()
            else:
                place[rows(x), :] = chosen()
            at[f] = gather_start(place, x, xp, xm)

        def forward():
            at[f] = gather_pass(place, x, xp, xm, at[f])

        def done():
            for copy in at[f]:
                copy.wait_recv()
            store_split(pair, (h,), place[...])

        steps.update({
            name + ".start": start, name + ".merge": merge, name + ".home": end, name + ".shift": shift,
            name + ".piece": piece, name + ".pass": forward, name + ".done": done,
        })

    def right_unit(s, h, name):
        f, g, here = 4 + s * 2 + h, s * 2 + h, pl.ds(h * 256, 256)
        both = (first_right, second_right)[s]
        place = both.at[core, h]
        pair = (fr_split, sr_split)[s]
        mates = []

        def ref(where):
            return right_pick.at[g, where]

        def value(where):
            return right_pick[g, where, :]

        def swap():
            at[f] = send(right.at[0, 0, s, 1 - core, :, here], right_swap.at[g], mate)

        def start():
            need(load_right[s])
            at[f].wait_recv()
            right_pick[g] = jnp.where(rc[s] == core, right_own[s, :, here], right_swap[g])
            at[f] = scatter_start(ref, y, yp, ym, f)

        def merge():
            at[f] = scatter_merge(value, y, yp, ym, f, ry[s], at[f])

        def end():
            scatter_end(value, y, f, ry[s], at[f])
            at[f] = (
                send(home.at[f, pl.ds(0, HALF)], right_z.at[g, 0], zp),
                send(home.at[f, pl.ds(HALF, HALF)], right_z.at[g, 1], zm),
            )

        def pass_on():
            one, two = at[f]
            one.wait_recv()
            relay[g, 0] = jnp.where(rz[s] == zh, home[f, HALF:], right_z[g, 0])
            three = send(relay.at[g, 0], right_z.at[g, 2], zp)
            two.wait_recv()
            relay[g, 1] = jnp.where(rz[s] == zh, home[f, :HALF], right_z[g, 1])
            at[f] = (three, send(relay.at[g, 1], right_z.at[g, 3], zm))

        def chosen():
            for copy in at[f]:
                copy.wait_recv()
            own, behind, ahead = rz[s] == zh, rz[s] == turn(zh, -1), rz[s] == turn(zh, 1)
            plus_one, minus_one, plus_two, minus_two = (right_z[g, k] for k in range(4))
            low = jnp.where(behind, plus_one, jnp.where(ahead, minus_two, plus_two))
            high = jnp.where(behind, plus_two, jnp.where(ahead, minus_one, minus_two))
            return jnp.where(own, home[f, :HALF], low), jnp.where(own, home[f, HALF:], high)

        def shift():
            aside[1, :HALF], aside[1, HALF:] = chosen()
            at[f] = describe(aside.at[1], second_right.at[1, 1, rows(y)], col_next)
            at["shift"] = at[f]

            @pl.when(core == 1)
            def _():
                at[f].start()

            @pl.when(core == 0)
            def _():
                place[rows(y), :] = aside[1]

        def piece():
            if (s, h) == (1, 1):

                @pl.when(core == 1)
                def _():
                    at[f].wait_recv()
            else:
                place[rows(y, 0), :], place[rows(y, 1), :] = chosen()
            at[f] = gather_start(place, y, yp, ym)
            mates.append(to_mate(place, rows(y)))

        def forward():
            at[f] = gather_pass(place, y, yp, ym, at[f])
            mates.append(to_mate(place, rows(turn(y, -1))))
            mates.append(to_mate(place, rows(turn(y, 1))))

        def last():
            for copy in at[f]:
                copy.wait_recv()
            mates.append(to_mate(place, rows(turn(y, 2))))

        def done():
            for copy in mates:
                copy.wait_recv()
            for m in range(2):
                store_split(pair, (m, h), both[m, h])

        steps.update({
            name + ".swap": swap, name + ".start": start, name + ".merge": merge, name + ".home": end,
            name + ".relay": pass_on, name + ".shift": shift, name + ".piece": piece, name + ".pass": forward,
            name + ".last": last, name + ".done": done,
        })

    for s in range(2):
        for h in range(2):
            tail = "12"[s] + "ab"[h]
            left_unit(s, h, "L" + tail)
            right_unit(s, h, "R" + tail)

    def border_send(t):
        up, down = cur.at[t, pl.ds(0, 256)], cur.at[t, pl.ds(256, 256)]
        to_prev = describe(up, below.at[t], row_prev)
        to_next = describe(down, above.at[t], row_next)
        last = [
            describe(cur.at[t, pl.ds(256, 128)], hop.at[t, 0], zp),
            describe(cur.at[t, pl.ds(384, 128)], hop.at[t, 1], across),
        ]
        first = [
            describe(cur.at[t, pl.ds(0, 128)], hop.at[t, 0], zm),
            describe(cur.at[t, pl.ds(128, 128)], hop.at[t, 1], across),
        ]
        last_on = [
            describe(hop.at[t, 0], above.at[t, pl.ds(0, 128)], across),
            describe(hop.at[t, 1], below.at[t, pl.ds(128, 128)], zm),
        ]
        first_on = [
            describe(hop.at[t, 0], below.at[t, pl.ds(0, 128)], across),
            describe(hop.at[t, 1], above.at[t, pl.ds(128, 128)], zp),
        ]

        @pl.when(~is_last)
        def _():
            to_next.start()

        @pl.when(~is_first)
        def _():
            to_prev.start()

        @pl.when(is_last)
        def _():
            for copy in last:
                copy.start()

        @pl.when(is_first)
        def _():
            for copy in first:
                copy.start()

        return to_prev, to_next, last, first, last_on, first_on

    def border_pass(copies):
        _, _, last, first, last_on, first_on = copies

        @pl.when(is_last)
        def _():
            last[0].wait_recv()
            last_on[0].start()
            first[1].wait_recv()
            last_on[1].start()

        @pl.when(is_first)
        def _():
            first[0].wait_recv()
            first_on[0].start()
            last[1].wait_recv()
            first_on[1].start()

    def border_wait(copies):
        to_prev, to_next, _, _, last_on, first_on = copies

        @pl.when(~is_last)
        def _():
            to_prev.wait_recv()

        @pl.when(~is_first)
        def _():
            to_next.wait_recv()

        @pl.when(is_last)
        def _():
            first_on[0].wait_recv()
            last_on[1].wait_recv()

        @pl.when(is_first)
        def _():
            last_on[0].wait_recv()
            first_on[1].wait_recv()

    def border_end(copies):
        to_prev, to_next, last, first, last_on, first_on = copies

        @pl.when(~is_last)
        def _():
            to_next.wait_send()

        @pl.when(~is_first)
        def _():
            to_prev.wait_send()

        @pl.when(is_last)
        def _():
            for copy in last + last_on:
                copy.wait_send()

        @pl.when(is_first)
        def _():
            for copy in first + first_on:
                copy.wait_send()

    top_stays, bottom_stays = row == 0, row == 31
    row_swaps, col_swaps = {}, {}

    def win_step():
        need(load_win)
        store_split(win_split, (slice(None), slice(None)), win[...])

    def first_rows(t):
        cols = slice(t * 256, t * 256 + 256)
        for h in range(2):
            part = slice(h * 256, h * 256 + 256)
            value = product(
                (fl_split[0, h], fl_split[1, h]), (win_split[0, :, cols], win_split[1, :, cols]), 0
            )
            cur[t, part] = value
            store_split(cur_split, (t, part), value)
        row_swaps[t] = border_send(t)

    def second_rows(t):
        border_wait(row_swaps[t])
        cols = slice(t * 256, t * 256 + 256)
        top = (cur_split[0, t, :256], cur_split[1, t, :256])
        bottom = (cur_split[0, t, 256:], cur_split[1, t, 256:])

        def blend(h, upper, lower):
            one = product((sl_split[0, h, :256], sl_split[1, h, :256]), upper, 0)
            return one + product((sl_split[0, h, 256:], sl_split[1, h, 256:]), lower, 0)

        new_bottom = blend(0, bottom, split(below[t]))
        new_top = blend(1, split(above[t]), top)
        new_top = jnp.where(top_stays, cur[t, :256], new_top)
        new_bottom = jnp.where(bottom_stays, cur[t, 256:], new_bottom)
        store_split(mid_split, (slice(0, 256), cols), new_top)
        store_split(mid_split, (slice(256, 512), cols), new_bottom)

    def first_cols(t):
        m, h = t // 2, t % 2
        band = slice(m * 512, m * 512 + 512)
        value = product(
            (mid_split[0, :, band], mid_split[1, :, band]), (fr_split[0, m, h], fr_split[1, m, h])
        )
        nxt[t] = value
        store_split(nxt_split, (t,), value)
        if t == 0:
            col_swaps[t] = send(nxt.at[0], from_right, col_prev)
        if t == 3:
            col_swaps[t] = send(nxt.at[3], from_left, col_next)

    def term(value, m, h, k):
        part = slice(k * 256, k * 256 + 256)
        return product(value, (sr_split[0, m, h, part], sr_split[1, m, h, part]))

    def kept(t):
        return nxt_split[0, t], nxt_split[1, t]

    def middle():
        for h in range(2):
            result[:, 256 + h * 256 : 512 + h * 256] = term(kept(1), 0, h, 0) + term(kept(2), 0, h, 1)

    def right_edge():
        edge = term(kept(3), 1, 0, 0)
        col_swaps[0].wait_recv()
        edge = edge + term(split(from_right[...]), 1, 0, 1)
        result[:, 768:] = jnp.where(col == 7, nxt[3], edge)

    def left_edge():
        edge = term(kept(0), 1, 1, 1)
        col_swaps[3].wait_recv()
        edge = edge + term(split(from_left[...]), 1, 1, 0)
        result[:, :256] = jnp.where(col == 0, nxt[0], edge)

    steps.update({"win": win_step, "mid": middle, "edgeR": right_edge, "edgeL": left_edge})
    for t in range(4):
        steps.update({
            "x1." + str(t): functools.partial(first_rows, t), "x2." + str(t): functools.partial(second_rows, t),
            "x3." + str(t): functools.partial(first_cols, t),
            "hop" + str(t): lambda t=t: border_pass(row_swaps[t]),
        })
    for name in ORDER:
        steps[name]()
    store = pltpu.make_async_copy(result, out, local_sem.at[len(loads)])
    store.start()
    for copy in sent:
        copy.wait_send()
    for copies in row_swaps.values():
        border_end(copies)

    @pl.when(core == 1)
    def _():
        at["shift"].wait_send()

    store.wait()


def place(src, dst, held, in_sem, out_sem):
    parts = [pl.ds(k * 64, 64) for k in range(8)]
    reads = [pltpu.make_async_copy(src.at[p], held.at[p], in_sem.at[k]) for k, p in enumerate(parts)]
    writes = [pltpu.make_async_copy(held.at[p], dst.at[p], out_sem.at[k]) for k, p in enumerate(parts)]
    for copy in reads:
        copy.start()
    for read, write in zip(reads, writes):
        read.wait()
        write.start()
    for copy in writes:
        copy.wait()


def shards(window, left_slots, right_slots, left_owner, right_owner):
    scratch = [
        pltpu.VMEM((512, 1024), F32),
        pltpu.VMEM((2, 512, 512), F32),
        pltpu.VMEM((2, 512, 512), F32),
        pltpu.VMEM((4, 512, 256), F32),
        pltpu.VMEM((4, 512, 256), F32),
        pltpu.VMEM((2, 512, 256), F32),
        pltpu.VMEM((2, 512, 256), F32),
        pltpu.VMEM((2, 2, 512, 256), F32),
        pltpu.VMEM((2, 2, 512, 256), F32),
        pltpu.VMEM((8, 6, HALF, 256), F32),
        pltpu.VMEM((8, 2, HALF, 256), F32),
        pltpu.VMEM((8, PIECE, 256), F32),
        pltpu.VMEM((4, PIECE, 256), F32),
        pltpu.VMEM((4, 4, HALF, 256), F32),
        pltpu.VMEM((4, 2, HALF, 256), F32),
        pltpu.VMEM((2, PIECE, 256), F32),
        pltpu.VMEM((2, 512, 1024), BF16),
        pltpu.VMEM((2, 2, 512, 256), BF16),
        pltpu.VMEM((2, 2, 512, 256), BF16),
        pltpu.VMEM((2, 2, 2, 512, 256), BF16),
        pltpu.VMEM((2, 2, 2, 512, 256), BF16),
        pltpu.VMEM((2, 512, 1024), BF16),
        pltpu.VMEM((4, 512, 256), F32),
        pltpu.VMEM((2, 4, 512, 256), BF16),
        pltpu.VMEM((4, 256, 256), F32),
        pltpu.VMEM((4, 256, 256), F32),
        pltpu.VMEM((4, 2, 128, 256), F32),
        pltpu.VMEM((4, 512, 256), F32),
        pltpu.VMEM((2, 4, 512, 256), BF16),
        pltpu.VMEM((512, 256), F32),
        pltpu.VMEM((512, 256), F32),
        pltpu.VMEM((512, 1024), F32),
        pltpu.SemaphoreType.DMA((COPIES,)),
        pltpu.SemaphoreType.DMA((COPIES,)),
        pltpu.SemaphoreType.DMA((8,)),
    ]
    smem, hbm = pl.BlockSpec(memory_space=pltpu.SMEM), pl.BlockSpec(memory_space=pl.ANY)
    made = pl.pallas_call(
        kernel,
        name="far_update",
        out_shape=jax.ShapeDtypeStruct(window.shape, F32),
        in_specs=[smem, smem, hbm, hbm, hbm],
        out_specs=hbm,
        scratch_shapes=scratch,
        compiler_params=pltpu.CompilerParams(
            collective_id=0, has_side_effects=True, vmem_limit_bytes=58 * 2**20
        ),
    )(left_owner, right_owner, window, left_slots, right_slots)
    return pl.pallas_call(
        place,
        name="place",
        out_shape=jax.ShapeDtypeStruct(window.shape, F32),
        in_specs=[hbm],
        out_specs=hbm,
        scratch_shapes=[
            pltpu.VMEM(window.shape, F32),
            pltpu.SemaphoreType.DMA((8,)),
            pltpu.SemaphoreType.DMA((8,)),
        ],
    )(made)


def solution(mesh):
    in_specs = (
        P("row", "col"),
        P("row", "col", None, None, None, None),
        P("row", "col", None, None, None, None),
        P("row", None),
        P("col", None),
    )
    out_specs = P("row", "col")
    return jax.shard_map(shards, mesh=mesh, in_specs=in_specs, out_specs=out_specs, check_vma=False)
```

```python
import functools

import jax
import jax.numpy as jnp
from jax import lax
from jax.experimental import pallas as pl
from jax.experimental.pallas import tpu as pltpu
from jax.sharding import PartitionSpec as P

MESH = pl.DeviceIdType.MESH
F32, BF16 = jnp.float32, jnp.bfloat16
COPIES = 176
PIECE, HALF = 128, 64
ORDER = (
    "L1b.start", "R1b.swap", "win", "R1a.swap", "R2b.swap", "L1a.start", "R2a.swap", "R1b.start", "L1b.merge",
    "R1a.start", "L1a.merge", "L1b.home", "L2b.start", "R1b.merge", "L1a.home", "R1a.merge", "R2b.start",
    "L2a.start", "R1b.home", "L1b.piece", "R1a.home", "L2b.merge", "R2a.start", "R2b.merge", "R1b.relay",
    "L2a.merge", "L1a.piece", "L1b.pass", "L2b.home", "R2a.merge", "R1a.relay", "R1b.piece", "L1a.pass",
    "L2a.home", "L2b.shift", "R2b.home", "R1a.piece", "R1b.pass", "L1a.done", "L1b.done", "L2b.piece", "x1.0",
    "L2a.piece", "R1b.last", "R2a.home", "x1.1", "hop0", "x1.2", "R1a.pass", "L2b.pass", "R1b.done",
    "L2a.pass", "R2b.relay", "L2b.done", "x1.3", "hop1", "L2a.done", "hop2", "x2.0", "R1a.last", "R2a.relay",
    "R2b.shift", "hop3", "x2.1", "R1a.done", "x3.0", "R2b.piece", "x2.2", "R2a.piece", "x2.3", "x3.3",
    "R2b.pass", "R2a.pass", "R2b.last", "x3.2", "R2a.last", "x3.1", "R2b.done", "R2a.done", "mid", "edgeR",
    "edgeL",
)


def split(value):
    high = value.astype(BF16)
    return high, (value - high.astype(F32)).astype(BF16)


def product(a, b, contract_a=1):
    dims = (((contract_a,), (0,)), ((), ()))

    def dot(p, q):
        return lax.dot_general(p, q, dims, preferred_element_type=F32)

    return dot(a[0], b[0]) + (dot(a[0], b[1]) + dot(a[1], b[0]))


def kernel(
    left_owner, right_owner, window, left, right, out,
    win, left_own, right_own, right_give, right_swap, right_pick,
    first_left, second_left, first_right, second_right,
    arrive, merged, home, left_z, right_z, relay, aside,
    win_split, fl_split, sl_split, fr_split, sr_split,
    mid_split, cur, cur_split, above, below, hop, nxt, nxt_split, from_left, from_right,
    result, send_sem, recv_sem, local_sem,
):
    row, col = lax.axis_index("row"), lax.axis_index("col")
    zh, y, core = row // 8, (row // 2) % 4, row % 2
    zl, x = col // 4, col % 4

    def turn(v, d, n=4):
        return lax.rem(v + d + n, n)

    xp, xm = (row, zl * 4 + turn(x, 1)), (row, zl * 4 + turn(x, -1))
    zpair = (row, (1 - zl) * 4 + x)
    yp, ym = (zh * 8 + turn(y, 1) * 2 + core, col), (zh * 8 + turn(y, -1) * 2 + core, col)
    zp, zm = (turn(zh, 1) * 8 + y * 2 + core, col), (turn(zh, -1) * 8 + y * 2 + core, col)
    mate = (zh * 8 + y * 2 + 1 - core, col)
    row_next, row_prev = (turn(row, 1, 32), col), (turn(row, -1, 32), col)
    col_next, col_prev = (row, turn(col, 1, 8)), (row, turn(col, -1, 8))

    loads = []

    def load(src, dst):
        copy = pltpu.make_async_copy(src, dst, local_sem.at[len(loads)])
        copy.start()
        loads.append(copy)
        return copy

    load_left = [load(left.at[0, 0, s, 0], left_own.at[s]) for s in range(2)]
    load_give = [load(right.at[0, 0, s, 1 - core], right_give.at[s]) for s in range(2)]
    load_right = [load(right.at[0, 0, s, core], right_own.at[s]) for s in range(2)]
    load_win = load(window, win)
    loaded = []

    def need(copy):
        if not any(copy is other for other in loaded):
            copy.wait()
            loaded.append(copy)

    is_last, is_first = (y == 3) & (core == 1), (y == 0) & (core == 0)
    across = (zh * 8 + 7 - y * 2 - core, col)
    partners = (
        xp, xm, zpair, yp, ym, zp, zm, mate, row_next, row_prev, col_next, col_prev, across,
    )
    barrier = pltpu.get_barrier_semaphore()
    for partner in partners:
        pl.semaphore_signal(barrier, inc=1, device_id=partner, device_id_type=MESH)
    pl.semaphore_wait(barrier, len(partners))

    made = [0]
    sent = []

    def describe(src, dst, device):
        k = made[0]
        made[0] += 1
        return pltpu.make_async_remote_copy(
            src_ref=src, dst_ref=dst, send_sem=send_sem.at[k], recv_sem=recv_sem.at[k],
            device_id=device, device_id_type=MESH,
        )

    def send(src, dst, device):
        copy = describe(src, dst, device)
        copy.start()
        sent.append(copy)
        return copy

    def rows(piece, part=None):
        if part is None:
            return pl.ds(pl.multiple_of(piece * PIECE, PIECE), PIECE)
        return pl.ds(pl.multiple_of(piece * PIECE + part * HALF, HALF), HALF)

    def scatter_start(ref, pos, plus, minus, f):
        far, ahead, behind = turn(pos, 2), turn(pos, 1), turn(pos, -1)
        return (
            send(ref(rows(far, 0)), arrive.at[f, 0], plus),
            send(ref(rows(far, 1)), arrive.at[f, 1], minus),
            send(ref(rows(ahead, 1)), arrive.at[f, 2], plus),
            send(ref(rows(behind, 0)), arrive.at[f, 3], minus),
        )

    def scatter_merge(value, pos, plus, minus, f, owner, copies):
        ahead, behind = turn(pos, 1), turn(pos, -1)
        copies[0].wait_recv()
        merged[f, 0] = jnp.where(owner == behind, arrive[f, 0], value(rows(ahead, 0)))
        one = send(merged.at[f, 0], arrive.at[f, 4], plus)
        copies[1].wait_recv()
        merged[f, 1] = jnp.where(owner == ahead, arrive[f, 1], value(rows(behind, 1)))
        two = send(merged.at[f, 1], arrive.at[f, 5], minus)
        return copies + (one, two)

    def scatter_end(value, pos, f, owner, copies):
        ahead, behind = turn(pos, 1), turn(pos, -1)
        for copy in copies[2:]:
            copy.wait_recv()
        low = jnp.where(owner == ahead, arrive[f, 3], arrive[f, 4])
        home[f, :HALF] = jnp.where(owner == pos, value(rows(pos, 0)), low)
        high = jnp.where(owner == behind, arrive[f, 2], arrive[f, 5])
        home[f, HALF:] = jnp.where(owner == pos, value(rows(pos, 1)), high)

    def gather_start(ref, pos, plus, minus):
        own = ref.at[rows(pos)]
        return (send(own, own, plus), send(own, own, minus))

    def gather_pass(ref, pos, plus, minus, copies):
        ahead, behind = turn(pos, 1), turn(pos, -1)
        copies[0].wait_recv()
        low = ref.at[rows(behind, 0)]
        one = send(low, low, plus)
        copies[1].wait_recv()
        high = ref.at[rows(ahead, 1)]
        return (one, send(high, high, minus))

    def to_mate(ref, where):
        part = ref.at[where]
        return send(part, part, mate)

    def store_split(pair, where, value):
        high, low = split(value)
        pair[(0, *where)] = high
        pair[(1, *where)] = low

    lown = [left_owner[0, s] for s in range(2)]
    rown = [right_owner[0, s] for s in range(2)]
    lx, lz = [v % 4 for v in lown], [v // 4 for v in lown]
    ry, rc, rz = [(v // 2) % 4 for v in rown], [v % 2 for v in rown], [v // 8 for v in rown]
    steps = {}
    at = {}

    def left_unit(s, h, name):
        f, here = s * 2 + h, pl.ds(h * 256, 256)
        place = (first_left, second_left)[s].at[h]
        pair = (fl_split, sl_split)[s]

        def ref(where):
            return left_own.at[s, where, here]

        def value(where):
            return left_own[s, where, here]

        def start():
            need(load_left[s])
            at[f] = scatter_start(ref, x, xp, xm, f)

        def merge():
            need(load_left[s])
            at[f] = scatter_merge(value, x, xp, xm, f, lx[s], at[f])

        def end():
            scatter_end(value, x, f, lx[s], at[f])
            at[f] = send(home.at[f], left_z.at[f], zpair)

        def chosen():
            at[f].wait_recv()
            return jnp.where(lz[s] == zl, home[f], left_z[f])

        def shift():
            aside[0] = chosen()
            at[f] = send(aside.at[0], place.at[rows(x)], row_next)

        def piece():
            if (s, h) == (1, 1):
                at[f].wait_recv()
            else:
                place[rows(x), :] = chosen()
            at[f] = gather_start(place, x, xp, xm)

        def forward():
            at[f] = gather_pass(place, x, xp, xm, at[f])

        def done():
            for copy in at[f]:
                copy.wait_recv()
            store_split(pair, (h,), place[...])

        steps.update({
            name + ".start": start, name + ".merge": merge, name + ".home": end, name + ".shift": shift,
            name + ".piece": piece, name + ".pass": forward, name + ".done": done,
        })

    def right_unit(s, h, name):
        f, g, here = 4 + s * 2 + h, s * 2 + h, pl.ds(h * 256, 256)
        both = (first_right, second_right)[s]
        place = both.at[core, h]
        pair = (fr_split, sr_split)[s]
        mates = []

        def ref(where):
            return right_pick.at[g, where]

        def value(where):
            return right_pick[g, where, :]

        def swap():
            need(load_give[s])
            at[f] = send(right_give.at[s, :, here], right_swap.at[g], mate)

        def start():
            need(load_right[s])
            at[f].wait_recv()
            right_pick[g] = jnp.where(rc[s] == core, right_own[s, :, here], right_swap[g])
            at[f] = scatter_start(ref, y, yp, ym, f)

        def merge():
            at[f] = scatter_merge(value, y, yp, ym, f, ry[s], at[f])

        def end():
            scatter_end(value, y, f, ry[s], at[f])
            at[f] = (
                send(home.at[f, pl.ds(0, HALF)], right_z.at[g, 0], zp),
                send(home.at[f, pl.ds(HALF, HALF)], right_z.at[g, 1], zm),
            )

        def pass_on():
            one, two = at[f]
            one.wait_recv()
            relay[g, 0] = jnp.where(rz[s] == zh, home[f, HALF:], right_z[g, 0])
            three = send(relay.at[g, 0], right_z.at[g, 2], zp)
            two.wait_recv()
            relay[g, 1] = jnp.where(rz[s] == zh, home[f, :HALF], right_z[g, 1])
            at[f] = (three, send(relay.at[g, 1], right_z.at[g, 3], zm))

        def chosen():
            for copy in at[f]:
                copy.wait_recv()
            own, behind, ahead = rz[s] == zh, rz[s] == turn(zh, -1), rz[s] == turn(zh, 1)
            plus_one, minus_one, plus_two, minus_two = (right_z[g, k] for k in range(4))
            low = jnp.where(behind, plus_one, jnp.where(ahead, minus_two, plus_two))
            high = jnp.where(behind, plus_two, jnp.where(ahead, minus_one, minus_two))
            return jnp.where(own, home[f, :HALF], low), jnp.where(own, home[f, HALF:], high)

        def shift():
            aside[1, :HALF], aside[1, HALF:] = chosen()
            at[f] = describe(aside.at[1], second_right.at[1, 1, rows(y)], col_next)
            at["shift"] = at[f]

            @pl.when(core == 1)
            def _():
                at[f].start()

            @pl.when(core == 0)
            def _():
                place[rows(y), :] = aside[1]

        def piece():
            if (s, h) == (1, 1):

                @pl.when(core == 1)
                def _():
                    at[f].wait_recv()
            else:
                place[rows(y, 0), :], place[rows(y, 1), :] = chosen()
            at[f] = gather_start(place, y, yp, ym)
            mates.append(to_mate(place, rows(y)))

        def forward():
            at[f] = gather_pass(place, y, yp, ym, at[f])
            mates.append(to_mate(place, rows(turn(y, -1))))
            mates.append(to_mate(place, rows(turn(y, 1))))

        def last():
            for copy in at[f]:
                copy.wait_recv()
            mates.append(to_mate(place, rows(turn(y, 2))))

        def done():
            for copy in mates:
                copy.wait_recv()
            for m in range(2):
                store_split(pair, (m, h), both[m, h])

        steps.update({
            name + ".swap": swap, name + ".start": start, name + ".merge": merge, name + ".home": end,
            name + ".relay": pass_on, name + ".shift": shift, name + ".piece": piece, name + ".pass": forward,
            name + ".last": last, name + ".done": done,
        })

    for s in range(2):
        for h in range(2):
            tail = "12"[s] + "ab"[h]
            left_unit(s, h, "L" + tail)
            right_unit(s, h, "R" + tail)

    def border_send(t):
        up, down = cur.at[t, pl.ds(0, 256)], cur.at[t, pl.ds(256, 256)]
        to_prev = describe(up, below.at[t], row_prev)
        to_next = describe(down, above.at[t], row_next)
        last = [
            describe(cur.at[t, pl.ds(256, 128)], hop.at[t, 0], zp),
            describe(cur.at[t, pl.ds(384, 128)], hop.at[t, 1], across),
        ]
        first = [
            describe(cur.at[t, pl.ds(0, 128)], hop.at[t, 0], zm),
            describe(cur.at[t, pl.ds(128, 128)], hop.at[t, 1], across),
        ]
        last_on = [
            describe(hop.at[t, 0], above.at[t, pl.ds(0, 128)], across),
            describe(hop.at[t, 1], below.at[t, pl.ds(128, 128)], zm),
        ]
        first_on = [
            describe(hop.at[t, 0], below.at[t, pl.ds(0, 128)], across),
            describe(hop.at[t, 1], above.at[t, pl.ds(128, 128)], zp),
        ]

        @pl.when(~is_last)
        def _():
            to_next.start()

        @pl.when(~is_first)
        def _():
            to_prev.start()

        @pl.when(is_last)
        def _():
            for copy in last:
                copy.start()

        @pl.when(is_first)
        def _():
            for copy in first:
                copy.start()

        return to_prev, to_next, last, first, last_on, first_on

    def border_pass(copies):
        _, _, last, first, last_on, first_on = copies

        @pl.when(is_last)
        def _():
            last[0].wait_recv()
            last_on[0].start()
            first[1].wait_recv()
            last_on[1].start()

        @pl.when(is_first)
        def _():
            first[0].wait_recv()
            first_on[0].start()
            last[1].wait_recv()
            first_on[1].start()

    def border_wait(copies):
        to_prev, to_next, _, _, last_on, first_on = copies

        @pl.when(~is_last)
        def _():
            to_prev.wait_recv()

        @pl.when(~is_first)
        def _():
            to_next.wait_recv()

        @pl.when(is_last)
        def _():
            first_on[0].wait_recv()
            last_on[1].wait_recv()

        @pl.when(is_first)
        def _():
            last_on[0].wait_recv()
            first_on[1].wait_recv()

    def border_end(copies):
        to_prev, to_next, last, first, last_on, first_on = copies

        @pl.when(~is_last)
        def _():
            to_next.wait_send()

        @pl.when(~is_first)
        def _():
            to_prev.wait_send()

        @pl.when(is_last)
        def _():
            for copy in last + last_on:
                copy.wait_send()

        @pl.when(is_first)
        def _():
            for copy in first + first_on:
                copy.wait_send()

    top_stays, bottom_stays = row == 0, row == 31
    row_swaps, col_swaps = {}, {}

    def win_step():
        need(load_win)
        store_split(win_split, (slice(None), slice(None)), win[...])

    def first_rows(t):
        cols = slice(t * 256, t * 256 + 256)
        for h in range(2):
            part = slice(h * 256, h * 256 + 256)
            value = product(
                (fl_split[0, h], fl_split[1, h]), (win_split[0, :, cols], win_split[1, :, cols]), 0
            )
            cur[t, part] = value
            store_split(cur_split, (t, part), value)
        row_swaps[t] = border_send(t)

    def second_rows(t):
        border_wait(row_swaps[t])
        cols = slice(t * 256, t * 256 + 256)
        top = (cur_split[0, t, :256], cur_split[1, t, :256])
        bottom = (cur_split[0, t, 256:], cur_split[1, t, 256:])

        def blend(h, upper, lower):
            one = product((sl_split[0, h, :256], sl_split[1, h, :256]), upper, 0)
            return one + product((sl_split[0, h, 256:], sl_split[1, h, 256:]), lower, 0)

        new_bottom = blend(0, bottom, split(below[t]))
        new_top = blend(1, split(above[t]), top)
        new_top = jnp.where(top_stays, cur[t, :256], new_top)
        new_bottom = jnp.where(bottom_stays, cur[t, 256:], new_bottom)
        store_split(mid_split, (slice(0, 256), cols), new_top)
        store_split(mid_split, (slice(256, 512), cols), new_bottom)

    def first_cols(t):
        m, h = t // 2, t % 2
        band = slice(m * 512, m * 512 + 512)
        value = product(
            (mid_split[0, :, band], mid_split[1, :, band]), (fr_split[0, m, h], fr_split[1, m, h])
        )
        nxt[t] = value
        store_split(nxt_split, (t,), value)
        if t == 0:
            col_swaps[t] = send(nxt.at[0], from_right, col_prev)
        if t == 3:
            col_swaps[t] = send(nxt.at[3], from_left, col_next)

    def term(value, m, h, k):
        part = slice(k * 256, k * 256 + 256)
        return product(value, (sr_split[0, m, h, part], sr_split[1, m, h, part]))

    def kept(t):
        return nxt_split[0, t], nxt_split[1, t]

    def middle():
        for h in range(2):
            result[:, 256 + h * 256 : 512 + h * 256] = term(kept(1), 0, h, 0) + term(kept(2), 0, h, 1)

    def right_edge():
        edge = term(kept(3), 1, 0, 0)
        col_swaps[0].wait_recv()
        edge = edge + term(split(from_right[...]), 1, 0, 1)
        result[:, 768:] = jnp.where(col == 7, nxt[3], edge)

    def left_edge():
        edge = term(kept(0), 1, 1, 1)
        col_swaps[3].wait_recv()
        edge = edge + term(split(from_left[...]), 1, 1, 0)
        result[:, :256] = jnp.where(col == 0, nxt[0], edge)

    steps.update({"win": win_step, "mid": middle, "edgeR": right_edge, "edgeL": left_edge})
    for t in range(4):
        steps.update({
            "x1." + str(t): functools.partial(first_rows, t), "x2." + str(t): functools.partial(second_rows, t),
            "x3." + str(t): functools.partial(first_cols, t),
            "hop" + str(t): lambda t=t: border_pass(row_swaps[t]),
        })
    for name in ORDER:
        steps[name]()
    store = pltpu.make_async_copy(result, out, local_sem.at[len(loads)])
    store.start()
    for copy in sent:
        copy.wait_send()
    for copies in row_swaps.values():
        border_end(copies)

    @pl.when(core == 1)
    def _():
        at["shift"].wait_send()

    store.wait()


def place(src, dst, held, in_sem, out_sem):
    parts = [pl.ds(k * 64, 64) for k in range(8)]
    reads = [pltpu.make_async_copy(src.at[p], held.at[p], in_sem.at[k]) for k, p in enumerate(parts)]
    writes = [pltpu.make_async_copy(held.at[p], dst.at[p], out_sem.at[k]) for k, p in enumerate(parts)]
    for copy in reads:
        copy.start()
    for read, write in zip(reads, writes):
        read.wait()
        write.start()
    for copy in writes:
        copy.wait()


def shards(window, left_slots, right_slots, left_owner, right_owner):
    scratch = [
        pltpu.VMEM((512, 1024), F32),
        pltpu.VMEM((2, 512, 512), F32),
        pltpu.VMEM((2, 512, 512), F32),
        pltpu.VMEM((2, 512, 512), F32),
        pltpu.VMEM((4, 512, 256), F32),
        pltpu.VMEM((4, 512, 256), F32),
        pltpu.VMEM((2, 512, 256), F32),
        pltpu.VMEM((2, 512, 256), F32),
        pltpu.VMEM((2, 2, 512, 256), F32),
        pltpu.VMEM((2, 2, 512, 256), F32),
        pltpu.VMEM((8, 6, HALF, 256), F32),
        pltpu.VMEM((8, 2, HALF, 256), F32),
        pltpu.VMEM((8, PIECE, 256), F32),
        pltpu.VMEM((4, PIECE, 256), F32),
        pltpu.VMEM((4, 4, HALF, 256), F32),
        pltpu.VMEM((4, 2, HALF, 256), F32),
        pltpu.VMEM((2, PIECE, 256), F32),
        pltpu.VMEM((2, 512, 1024), BF16),
        pltpu.VMEM((2, 2, 512, 256), BF16),
        pltpu.VMEM((2, 2, 512, 256), BF16),
        pltpu.VMEM((2, 2, 2, 512, 256), BF16),
        pltpu.VMEM((2, 2, 2, 512, 256), BF16),
        pltpu.VMEM((2, 512, 1024), BF16),
        pltpu.VMEM((4, 512, 256), F32),
        pltpu.VMEM((2, 4, 512, 256), BF16),
        pltpu.VMEM((4, 256, 256), F32),
        pltpu.VMEM((4, 256, 256), F32),
        pltpu.VMEM((4, 2, 128, 256), F32),
        pltpu.VMEM((4, 512, 256), F32),
        pltpu.VMEM((2, 4, 512, 256), BF16),
        pltpu.VMEM((512, 256), F32),
        pltpu.VMEM((512, 256), F32),
        pltpu.VMEM((512, 1024), F32),
        pltpu.SemaphoreType.DMA((COPIES,)),
        pltpu.SemaphoreType.DMA((COPIES,)),
        pltpu.SemaphoreType.DMA((8,)),
    ]
    smem, hbm = pl.BlockSpec(memory_space=pltpu.SMEM), pl.BlockSpec(memory_space=pl.ANY)
    made = pl.pallas_call(
        kernel,
        name="far_update",
        out_shape=jax.ShapeDtypeStruct(window.shape, F32),
        in_specs=[smem, smem, hbm, hbm, hbm],
        out_specs=hbm,
        scratch_shapes=scratch,
        compiler_params=pltpu.CompilerParams(
            collective_id=0, has_side_effects=True, vmem_limit_bytes=58 * 2**20
        ),
    )(left_owner, right_owner, window, left_slots, right_slots)
    return pl.pallas_call(
        place,
        name="place",
        out_shape=jax.ShapeDtypeStruct(window.shape, F32),
        in_specs=[hbm],
        out_specs=hbm,
        scratch_shapes=[
            pltpu.VMEM(window.shape, F32),
            pltpu.SemaphoreType.DMA((8,)),
            pltpu.SemaphoreType.DMA((8,)),
        ],
    )(made)


def solution(mesh):
    in_specs = (
        P("row", "col"),
        P("row", "col", None, None, None, None),
        P("row", "col", None, None, None, None),
        P("row", None),
        P("col", None),
    )
    out_specs = P("row", "col")
    return jax.shard_map(shards, mesh=mesh, in_specs=in_specs, out_specs=out_specs, check_vma=False)
```
